32 devices in a mesh: row: 8 (over y, x, core), col: 4 (over z).
Axes of the slice: x: 2, y: 2, z: 4, core: 2. Of those that a mesh axis runs over, the one named last changes fastest.
Arguments:
- embeddings: float32 [1024, 768], P(('row', 'col')), may hold values from -0.21650635 to 0.21650635
- sharpness: float32 [1024], P(('row', 'col')), may hold values from 0.5 to 4
- soft_labels: float32 [1024, 256], P(('row', 'col')), may hold values from 0 to 1
- seed_mask: int32 [1024], P(('row', 'col')), may hold values 0 or 1
- tile_mask: int32 [32, 32], P('row'), may hold values from 0 to 1, as said below
Outputs:
- spread_labels: float32 [1024, 256], P(('row', 'col'))
The draws below stay inside these ranges and needn't reach their ends.
Inputs may be any that keep to these rules, and one draw needn't show every extreme that they name: Every diagonal entry tile_mask[p, p] is 1.
All inputs are finite; a program needn't handle non-finite values. No bound on the sum of `seed_mask` on one device may be relied on, other than what follows from the above.
Results may differ from the reference program's by a relative error of at most 0.0003.
Values sent between devices are 32-bit elements; how exact they have to be, the bound alone decides.
A program may use at most 64 MiB of HBM per device.

```python
import math
import jax
import jax.numpy as jnp
from jax import lax

E = 768
LABELS = 256
PIECE = 32
ITERS = 3
PIECES = 32
DOCS = 1024
N_ROW = 8


def draw_tile_mask(key, part):
    key_rate, key_roll = jax.random.split(jax.random.fold_in(key, 17))
    density = jax.random.randint(key_rate, (PIECES, 1), 10, 26)
    rolled = jax.random.randint(key_roll, (PIECES, PIECES), 0, 100)
    diagonal = jnp.arange(PIECES)[:, None] == jnp.arange(PIECES)[None, :]
    return jnp.where(diagonal | (rolled < density), 1, 0).astype(jnp.int32)


def plant(drawn, stream_key, smallest, high):
    extent = drawn.shape
    place = [jax.random.randint(jax.random.fold_in(stream_key, axis), (), 0, extent[axis]) for axis in range(len(extent))]
    drawn = drawn.at[tuple(place)].set(smallest)
    longest = extent.index(max(extent))
    place[longest] = (place[longest] + 1) % extent[longest]
    return drawn.at[tuple(place)].set(high)


def block_scale(rng, shape, cuts, smallest, top_value):
    loudness = 1.0
    for axis_at, blocks in cuts:
        steps = jax.random.uniform(jax.random.fold_in(jax.random.fold_in(rng, 6), axis_at), (blocks,), jnp.float32, smallest / len(cuts), top_value / len(cuts))
        loudness = loudness * jnp.repeat(jnp.exp(steps), shape[axis_at] // blocks).reshape((-1,) + (1,) * (len(shape) - 1 - axis_at))
    return loudness


def centred(stream_key, dims, width, bound, pieces=(), kind=jnp.bfloat16):
    array = jax.random.normal(stream_key, dims, jnp.float32) * width
    if len(pieces) > 0:
        array = block_scale(stream_key, dims, pieces, -0.22, 0.18) * array
    return jnp.clip(array, min=-bound, max=bound).astype(kind)


def setup_inputs(seed: int = 0) -> dict:
    keys = jax.random.split(jax.random.key(seed), 6)
    embeddings = centred(keys[0], (DOCS, E), (E ** -0.5), 0.21650635, ((0, 32),), jnp.float32)
    sharpness = jnp.clip(jnp.exp(math.log(4.0) - 2.0794415 * jax.random.uniform(keys[1], (DOCS,), jnp.float32) ** block_scale(keys[1], (DOCS,), ((0, 32),), -0.2, 0.2)), 0.5, 4.0)
    soft_labels = jnp.clip(1.0 * jax.random.uniform(keys[2], (DOCS, LABELS), jnp.float32) ** block_scale(keys[2], (DOCS, LABELS), ((0, 32),), -0.2, 0.2), 0.0, 1.0)
    seed_mask = plant((jax.random.randint(keys[3], (DOCS,), 0, 4) < 1).astype(jnp.int32), jax.random.fold_in(keys[3], 1), 0, 1)
    tile_mask = draw_tile_mask(jax.random.fold_in(keys[5], 71), 0)
    return dict(embeddings=embeddings, sharpness=sharpness, soft_labels=soft_labels, seed_mask=seed_mask, tile_mask=tile_mask)


def reference(embeddings, sharpness, soft_labels, seed_mask, tile_mask):
    seeded = seed_mask.astype(jnp.float32)[:, None] * soft_labels
    squares = jnp.sum(embeddings * embeddings, axis=1)
    block_rows = DOCS // N_ROW
    piece_rows = block_rows // PIECE

    def block_update(labels, index):
        start = (index * block_rows).astype(jnp.int32)
        rows = lax.dynamic_slice_in_dim(embeddings, start, block_rows, 0)
        row_squares = lax.dynamic_slice_in_dim(squares, start, block_rows, 0)
        row_width = lax.dynamic_slice_in_dim(sharpness, start, block_rows, 0)
        piece_mask = lax.dynamic_slice_in_dim(tile_mask, (index * piece_rows).astype(jnp.int32), piece_rows, 0)
        full_mask = jnp.broadcast_to(piece_mask[:, None, :, None], (piece_rows, PIECE, PIECES, PIECE))
        full_mask = full_mask.reshape(block_rows, DOCS).astype(jnp.float32)
        cross = jnp.dot(rows, embeddings.T, precision=lax.Precision.HIGHEST, preferred_element_type=jnp.float32)
        distance = row_squares[:, None] + squares[None, :] - 2.0 * cross
        weights = jnp.exp(-(distance * row_width[:, None] * sharpness[None, :])) * full_mask
        partial_value = jnp.dot(weights, labels, precision=lax.Precision.HIGHEST, preferred_element_type=jnp.float32)
        return partial_value, jnp.sum(weights, axis=1)

    labels = seeded
    for iteration in range(ITERS):
        partial_value, degree = lax.map(lambda index: block_update(labels, index), jnp.arange(N_ROW, dtype=jnp.int32))
        partial_value = partial_value.reshape(DOCS, LABELS)
        degree = degree.reshape(DOCS)
        labels = 0.9 * partial_value / degree[:, None] + 0.1 * seeded
    return labels
```

```python
import functools

import jax
import jax.numpy as jnp
from jax import lax
from jax.experimental import pallas as pl
from jax.experimental.pallas import tpu as pltpu
from jax.sharding import PartitionSpec as P

ITERS = 3
MESH = pl.DeviceIdType.MESH
EXACT = lax.Precision.HIGHEST
AUX = 8


def dot(a, b, a_dim=1, b_dim=0):
    return lax.dot_general(
        a, b, (((a_dim,), (b_dim,)), ((), ())), precision=EXACT, preferred_element_type=jnp.float32
    )


def iota(shape, dim):
    return lax.broadcasted_iota(jnp.int32, shape, dim)


def to_column(line):
    n = line.shape[1]
    eye = iota((n, n), 0) == iota((n, n), 1)
    return jnp.sum(jnp.where(eye, jnp.broadcast_to(line, (n, n)), 0.0), axis=1, keepdims=True)


def kernel(
    chips, cols, emb_ref, sharp_ref, soft_ref, seed_ref, tile_ref, out_ref,
    row_emb, col_emb, row_aux, mask_buf, first, later, part, summed, last_part, last, weights, send,
    row_sem, col_sem, aux_sem, mask_sem, first_sem, later_sem, sum_sem, last_sem, send_sem,
):
    piece, width = emb_ref.shape
    half = soft_ref.shape[1] // 2
    rows = 2 * chips
    r, z = lax.axis_index("row"), lax.axis_index("col")
    chip, core = r // 2, lax.rem(r, 2)
    twin = r + 1 - 2 * core
    mine = 2 * z + core

    others_z = [lax.rem(z + d, cols) for d in range(1, cols)]
    others_chip = [lax.rem(chip + d, chips) for d in range(1, chips)]
    peers = [(twin, z)]
    peers += [(2 * chip + k, other) for other in others_z for k in range(2)]
    peers += [(2 * other + k, z) for other in others_chip for k in range(2)]

    barrier = pltpu.get_barrier_semaphore()
    for peer in peers:
        pl.semaphore_signal(barrier, inc=1, device_id=peer, device_id_type=MESH)

    sharp = sharp_ref[...]
    seeded = to_column(seed_ref[...].astype(jnp.float32)) * soft_ref[...]
    aux = jnp.concatenate([sharp, jnp.zeros((1, 128 - piece), jnp.float32)], axis=1)
    aux = jnp.broadcast_to(aux, (AUX, 128))
    row_aux[mine] = aux
    for k in range(2):
        send[k, :piece] = seeded[:, k * half : (k + 1) * half]
        send[k, piece:, :] = jnp.broadcast_to(aux[:, :1], (AUX, half)) if half < 128 else jnp.concatenate(
            [aux] + [jnp.zeros((AUX, half - 128), jnp.float32)] * (half > 128), axis=1
        )
    mask_buf[core] = jnp.zeros(mask_buf.shape[1:], jnp.float32)
    mask_buf[core, : tile_ref.shape[0], : tile_ref.shape[1]] = tile_ref[...].astype(jnp.float32)
    pl.semaphore_wait(barrier, len(peers))

    sent = []

    def push(src, dst, recv, peer):
        copy = pltpu.make_async_remote_copy(
            src_ref=src, dst_ref=dst, send_sem=send_sem.at[len(sent)], recv_sem=recv,
            device_id=peer, device_id_type=MESH,
        )
        copy.start()
        sent.append(copy)

    def arrived(dst, recv):
        pltpu.make_async_remote_copy(
            src_ref=dst, dst_ref=dst, send_sem=send_sem.at[0], recv_sem=recv,
            device_id=(twin, z), device_id_type=MESH,
        ).wait_recv()

    for other in others_z:
        push(emb_ref, row_emb.at[mine], row_sem.at[mine], (r, other))
    for other in others_chip:
        push(emb_ref, col_emb.at[r], col_sem.at[r], (2 * other + core, z))
    push(emb_ref, row_emb.at[mine], row_sem.at[mine], (twin, z))
    push(emb_ref, col_emb.at[r], col_sem.at[r], (twin, z))
    push(row_aux.at[mine], row_aux.at[mine], aux_sem.at[mine], (twin, z))
    for other in others_z:
        for k in range(2):
            push(row_aux.at[mine], row_aux.at[mine], aux_sem.at[mine], (2 * chip + k, other))
    push(send.at[1 - core], first.at[r], first_sem.at[r], (twin, z))
    for other in others_chip:
        for k in range(2):
            push(send.at[k], first.at[r], first_sem.at[r], (2 * other + k, z))
    push(mask_buf.at[core], mask_buf.at[core], mask_sem, (twin, z))

    row_emb[mine] = emb_ref[...]
    col_emb[r] = emb_ref[...]
    first[r] = send[core]

    for other in others_chip:
        slot = 2 * other + core
        arrived(col_emb.at[slot], col_sem.at[slot])
        push(col_emb.at[slot], col_emb.at[slot], col_sem.at[slot], (twin, z))
    for other in others_z:
        slot = 2 * other + core
        arrived(row_emb.at[slot], row_sem.at[slot])
        push(row_emb.at[slot], row_emb.at[slot], row_sem.at[slot], (twin, z))

    arrived(mask_buf.at[1 - core], mask_sem)
    for other in [z] + others_z:
        for k in range(2):
            slot = 2 * other + k
            if other is z:
                if k == 0:
                    arrived(row_aux.at[2 * z + 1 - core], aux_sem.at[2 * z + 1 - core])
            else:
                arrived(row_aux.at[slot], aux_sem.at[slot])
    arrived(first.at[twin], first_sem.at[twin])
    for other in others_chip:
        for k in range(2):
            arrived(first.at[2 * other + k], first_sem.at[2 * other + k])

    n_rows, n_cols = 2 * cols * piece, rows * piece
    mask_rows, tiles = 2 * mask_buf.shape[1], mask_buf.shape[2]
    wanted = (iota((tiles, n_cols), 1) // piece) * cols + z
    pick_cols = (iota((tiles, n_cols), 0) == wanted).astype(jnp.float32)
    col_mask = dot(mask_buf[...].reshape(mask_rows, tiles), pick_cols)
    line = first[:, piece:, :128].reshape(rows * AUX, 128)[:, :piece]
    at = iota((piece, n_cols), 1)
    spread = dot(line, (iota((piece, n_cols), 0) == lax.rem(at, piece)).astype(jnp.float32))
    at = iota((rows * AUX, n_cols), 1)
    keep = iota((rows * AUX, n_cols), 0) == (at // piece) * AUX
    col_sharp = jnp.sum(jnp.where(keep, spread, 0.0), axis=0, keepdims=True)

    arrived(col_emb.at[twin], col_sem.at[twin])
    for other in others_chip:
        slot = 2 * other + 1 - core
        arrived(col_emb.at[slot], col_sem.at[slot])
    theirs = col_emb[...].reshape(n_cols, width)
    col_squares = dot(jnp.ones((8, width), jnp.float32), theirs * theirs, 1, 1)[:1]
    arrived(row_emb.at[2 * z + 1 - core], row_sem.at[2 * z + 1 - core])
    for other in others_z:
        slot = 2 * other + 1 - core
        arrived(row_emb.at[slot], row_sem.at[slot])

    group = min(2 * cols, max(1, 256 // piece))

    def block(b):
        at = b * group
        ours = row_emb[pl.ds(at, group)].reshape(group * piece, width)
        cross = dot(ours, theirs, 1, 1)
        squares = jnp.sum(ours * ours, axis=1, keepdims=True)
        sharp_at = row_aux[pl.ds(at, group)]
        row_sharp = jnp.concatenate([to_column(sharp_at[g, :1, :piece]) for g in range(group)], axis=0)
        tile = iota((group * piece, mask_rows), 0) // piece + at
        wanted = lax.rem(tile, 2) * (mask_rows // 2) + tile // 2
        pick = (iota((group * piece, mask_rows), 1) == wanted).astype(jnp.float32)
        distance = squares + col_squares - 2.0 * cross
        value = jnp.exp(-(distance * row_sharp * col_sharp)) * dot(pick, col_mask)
        weights[pl.ds(b * group * piece, group * piece)] = value

    if group == 2 * cols:
        block(0)
    else:
        pl.loop(0, 2 * cols // group)(block)

    pair = 2 * piece
    kept = jnp.concatenate([first[2 * chip, :piece], first[2 * chip + 1, :piece]], axis=0)
    degree = None
    for step in range(ITERS):
        if step == 0:
            labels = first[:, :piece].reshape(n_cols, half)
        else:
            labels = later[step - 1].reshape(n_cols, half)
        if step < ITERS - 1:
            for c in range(cols):
                ours = weights[c * pair : (c + 1) * pair]
                part[step, c, :pair] = dot(ours, labels)
                if step == 0:
                    sums = dot(jnp.ones((AUX, n_cols), jnp.float32), ours, 1, 1)
                    part[step, c, pair:, :pair] = sums
            depth = pair + AUX if step == 0 else pair
            for other in others_z:
                push(
                    part.at[step, other, pl.ds(0, depth)], summed.at[step, z, pl.ds(0, depth)],
                    sum_sem.at[step, z], (r, other),
                )
            total = part[step, z, :depth]
            for other in others_z:
                arrived(summed.at[step, other, pl.ds(0, depth)], sum_sem.at[step, other])
                total = total + summed[step, other, :depth]
            if step == 0:
                degree = to_column(total[pair : pair + 1, :pair])
            new = 0.9 * total[:pair] / degree + 0.1 * kept
            later[step, chip] = new
            for other in others_chip:
                push(
                    later.at[step, chip], later.at[step, chip], later_sem.at[step, chip],
                    (2 * other + core, z),
                )
            for other in others_chip:
                arrived(later.at[step, other], later_sem.at[step, other])
        else:
            for c in range(cols):
                value = dot(weights[c * pair : (c + 1) * pair], labels)
                last_part[c] = value.reshape(2, piece, half)
            push(last_part.at[z, 1 - core], last.at[z, core], last_sem.at[z, core], (twin, z))
            for other in others_z:
                for k in range(2):
                    push(last_part.at[other, k], last.at[z, core], last_sem.at[z, core], (2 * chip + k, other))
            last[z, core] = last_part[z, core]
            arrived(last.at[z, 1 - core], last_sem.at[z, 1 - core])
            for other in others_z:
                for k in range(2):
                    arrived(last.at[other, k], last_sem.at[other, k])
            total = jnp.sum(last[...], axis=0)
            own = jnp.where(core == 0, degree[:piece], degree[piece:])
            for k in range(2):
                out_ref[:, k * half : (k + 1) * half] = (
                    0.9 * total[k] / own + 0.1 * send[k, :piece]
                )
    for copy in sent:
        copy.wait_send()


def round_up(n, m):
    return (n + m - 1) // m * m


def local(chips, cols, embeddings, sharpness, soft_labels, seed_mask, tile_mask):
    piece, width = embeddings.shape
    half = soft_labels.shape[1] // 2
    rows = 2 * chips
    tile_rows, tiles = round_up(tile_mask.shape[0], 8), round_up(tile_mask.shape[1], 128)
    pair = 2 * piece
    sends = (
        2 * (cols - 1) + 2 * (chips - 1) + 2 + 1 + 2 * (cols - 1) + 1 + 2 * (chips - 1) + 1
        + (ITERS - 1) * (cols + chips - 2) + 2 * cols - 1
    )
    f32, dma = jnp.float32, pltpu.SemaphoreType.DMA
    vmem = pl.BlockSpec(memory_space=pltpu.VMEM)
    return pl.pallas_call(
        functools.partial(kernel, chips, cols),
        out_shape=jax.ShapeDtypeStruct(soft_labels.shape, f32),
        in_specs=[vmem] * 5,
        out_specs=vmem,
        scratch_shapes=[
            pltpu.VMEM((2 * cols, piece, width), f32),
            pltpu.VMEM((rows, piece, width), f32),
            pltpu.VMEM((2 * cols, AUX, 128), f32),
            pltpu.VMEM((2, tile_rows, tiles), f32),
            pltpu.VMEM((rows, piece + AUX, half), f32),
            pltpu.VMEM((ITERS - 1, chips, pair, half), f32),
            pltpu.VMEM((ITERS - 1, cols, pair + AUX, half), f32),
            pltpu.VMEM((ITERS - 1, cols, pair + AUX, half), f32),
            pltpu.VMEM((cols, 2, piece, half), f32),
            pltpu.VMEM((cols, 2, piece, half), f32),
            pltpu.VMEM((2 * cols * piece, rows * piece), f32),
            pltpu.VMEM((2, piece + AUX, half), f32),
            dma((2 * cols,)),
            dma((rows,)),
            dma((2 * cols,)),
            dma(()),
            dma((rows,)),
            dma((ITERS - 1, chips)),
            dma((ITERS - 1, cols)),
            dma((cols, 2)),
            dma((sends,)),
        ],
        compiler_params=pltpu.CompilerParams(
            collective_id=0, has_side_effects=True, vmem_limit_bytes=48 * 1024 * 1024
        ),
    )(embeddings, sharpness.reshape(1, piece), soft_labels, seed_mask.reshape(1, piece), tile_mask)


def solution(mesh):
    return jax.shard_map(
        functools.partial(local, mesh.shape["row"] // 2, mesh.shape["col"]),
        mesh=mesh,
        in_specs=(
            P(("row", "col"), None),
            P(("row", "col")),
            P(("row", "col"), None),
            P(("row", "col")),
            P("row", None),
        ),
        out_specs=P(("row", "col"), None),
        check_vma=False,
    )
```

```python
import functools

import jax
import jax.numpy as jnp
from jax import lax
from jax.experimental import pallas as pl
from jax.experimental.pallas import tpu as pltpu
from jax.sharding import PartitionSpec as P

ITERS = 3
MESH = pl.DeviceIdType.MESH
EXACT = lax.Precision.HIGHEST
AUX = 8


def dot(a, b, a_dim=1, b_dim=0):
    return lax.dot_general(
        a, b, (((a_dim,), (b_dim,)), ((), ())), precision=EXACT, preferred_element_type=jnp.float32
    )


def iota(shape, dim):
    return lax.broadcasted_iota(jnp.int32, shape, dim)


def to_column(line):
    n = line.shape[1]
    eye = iota((n, n), 0) == iota((n, n), 1)
    return jnp.sum(jnp.where(eye, jnp.broadcast_to(line, (n, n)), 0.0), axis=1, keepdims=True)


def to_line(column):
    n = column.shape[0]
    eye = iota((n, n), 0) == iota((n, n), 1)
    return jnp.sum(jnp.where(eye, jnp.broadcast_to(column, (n, n)), 0.0), axis=0, keepdims=True)


def split(value):
    high = value.astype(jnp.bfloat16)
    return high, (value - high.astype(jnp.float32)).astype(jnp.bfloat16)


def quick(a, b, b_dim=0):
    return lax.dot_general(a, b, (((1,), (b_dim,)), ((), ())), preferred_element_type=jnp.float32)


def by_distance(n):
    return sorted(range(1, n), key=lambda d: (min(d, n - d), d))


def kernel(
    chips, cols, emb_ref, sharp_ref, soft_ref, seed_ref, tile_ref, out_ref,
    row_emb, col_emb, row_aux, mask_buf, first, later, part, summed, last_part, last,
    w_high, w_low, c_high, c_low, send, soft, sharp_in, seed_in, tile_in,
    row_sem, col_sem, aux_sem, mask_sem, first_sem, later_sem, sum_sem, last_sem, send_sem, load_sem,
):
    piece, width = emb_ref.shape
    half = soft_ref.shape[1] // 2
    rows = 2 * chips
    pair = 2 * piece
    r, z = lax.axis_index("row"), lax.axis_index("col")
    chip, core = r // 2, lax.rem(r, 2)
    twin = r + 1 - 2 * core
    mine = 2 * z + core

    others_z = [lax.rem(z + d, cols) for d in by_distance(cols)]
    others_chip = [lax.rem(chip + d, chips) for d in by_distance(chips)]
    peers = [(twin, z)]
    peers += [(2 * chip + k, other) for other in others_z for k in range(2)]
    peers += [(2 * other + k, z) for other in others_chip for k in range(2)]

    loads = []
    for src, dst in (
        (emb_ref, row_emb.at[mine]), (soft_ref, soft), (sharp_ref, sharp_in), (seed_ref, seed_in),
        (tile_ref, tile_in), (emb_ref, col_emb.at[r]),
    ):
        loads.append(pltpu.make_async_copy(src, dst, load_sem.at[len(loads)]))
        loads[-1].start()
    barrier = pltpu.get_barrier_semaphore()
    for peer in peers:
        pl.semaphore_signal(barrier, inc=1, device_id=peer, device_id_type=MESH)
    mask_buf[core] = jnp.zeros(mask_buf.shape[1:], jnp.float32)
    for load in loads:
        load.wait()

    sharp = sharp_in[...]
    aux = jnp.concatenate([sharp, jnp.zeros((1, 128 - piece), jnp.float32)], axis=1)
    aux = jnp.broadcast_to(aux, (AUX, 128))
    row_aux[mine] = aux
    mask_buf[core, : tile_ref.shape[0], : tile_ref.shape[1]] = tile_in[...].astype(jnp.float32)
    seeded = to_column(seed_in[...].astype(jnp.float32)) * soft[...]
    for k in range(2):
        send[k, :piece] = seeded[:, k * half : (k + 1) * half]
        send[k, piece:, :128] = aux
    first[r] = send[core]
    pl.semaphore_wait(barrier, len(peers))

    sent = []

    def push(src, dst, recv, peer):
        copy = pltpu.make_async_remote_copy(
            src_ref=src, dst_ref=dst, send_sem=send_sem.at[len(sent)], recv_sem=recv,
            device_id=peer, device_id_type=MESH,
        )
        copy.start()
        sent.append(copy)

    def arrived(dst, recv):
        pltpu.make_async_remote_copy(
            src_ref=dst, dst_ref=dst, send_sem=send_sem.at[0], recv_sem=recv,
            device_id=(twin, z), device_id_type=MESH,
        ).wait_recv()

    for other in others_z:
        push(row_emb.at[mine], row_emb.at[mine], row_sem.at[mine], (r, other))
    for other in others_chip:
        push(col_emb.at[r], col_emb.at[r], col_sem.at[r], (2 * other + core, z))
    push(col_emb.at[r], col_emb.at[r], col_sem.at[r], (twin, z))
    push(row_emb.at[mine], row_emb.at[mine], row_sem.at[mine], (twin, z))
    for other in others_chip:
        for k in range(2):
            push(send.at[k], first.at[r], first_sem.at[r], (2 * other + k, z))
    push(send.at[1 - core], first.at[r], first_sem.at[r], (twin, z))
    push(mask_buf.at[core], mask_buf.at[core], mask_sem, (twin, z))
    push(row_aux.at[mine], row_aux.at[mine], aux_sem.at[mine], (twin, z))
    for other in others_z:
        for k in range(2):
            push(row_aux.at[mine], row_aux.at[mine], aux_sem.at[mine], (2 * chip + k, other))

    for other in others_chip:
        slot = 2 * other + core
        arrived(col_emb.at[slot], col_sem.at[slot])
        push(col_emb.at[slot], col_emb.at[slot], col_sem.at[slot], (twin, z))

    def hand_on(other):
        slot = 2 * other + core
        arrived(row_emb.at[slot], row_sem.at[slot])
        push(row_emb.at[slot], row_emb.at[slot], row_sem.at[slot], (twin, z))

    n_cols = rows * piece
    mask_rows, tiles = 2 * mask_buf.shape[1], mask_buf.shape[2]
    arrived(first.at[twin], first_sem.at[twin])
    for other in others_chip:
        for k in range(2):
            arrived(first.at[2 * other + k], first_sem.at[2 * other + k])
    line = first[:, piece:, :128].reshape(rows * AUX, 128)[:, :piece]
    at = iota((piece, n_cols), 1)
    spread = dot(line, (iota((piece, n_cols), 0) == lax.rem(at, piece)).astype(jnp.float32))
    at = iota((rows * AUX, n_cols), 1)
    keep = iota((rows * AUX, n_cols), 0) == (at // piece) * AUX
    col_sharp = jnp.sum(jnp.where(keep, spread, 0.0), axis=0, keepdims=True)
    labels = jnp.concatenate(split(first[:, :piece].reshape(n_cols, half)), axis=1)

    arrived(mask_buf.at[1 - core], mask_sem)
    wanted = (iota((tiles, n_cols), 1) // piece) * cols + z
    pick_cols = (iota((tiles, n_cols), 0) == wanted).astype(jnp.bfloat16)
    col_mask = quick(mask_buf[...].reshape(mask_rows, tiles).astype(jnp.bfloat16), pick_cols)
    col_mask = col_mask.astype(jnp.bfloat16)

    arrived(row_aux.at[2 * z + 1 - core], aux_sem.at[2 * z + 1 - core])
    for other in others_z:
        for k in range(2):
            arrived(row_aux.at[2 * other + k], aux_sem.at[2 * other + k])

    arrived(col_emb.at[twin], col_sem.at[twin])
    for other in others_chip:
        slot = 2 * other + 1 - core
        arrived(col_emb.at[slot], col_sem.at[slot])
    theirs = col_emb[...].reshape(n_cols, width)
    c_high[...], c_low[...] = split(theirs)
    col_squares = dot(jnp.ones((8, width), jnp.float32), theirs * theirs, 1, 1)[:1]

    def product(c, labels):
        wide = quick(w_high[c], labels)
        return wide[:, :half] + wide[:, half:] + quick(w_low[c], labels[:, :half])

    def block(c):
        ours = row_emb[pl.ds(2 * c, 2)].reshape(pair, width)
        both = jnp.concatenate(split(ours), axis=0)
        by_high, by_low = quick(both, c_high[...], 1), quick(both, c_low[...], 1)
        cross = by_high[:pair] + (by_high[pair:] + by_low[:pair] + by_low[pair:])
        squares = jnp.sum(ours * ours, axis=1, keepdims=True)
        sharp_at = row_aux[pl.ds(2 * c, 2)]
        row_sharp = jnp.concatenate([to_column(sharp_at[g, :1, :piece]) for g in range(2)], axis=0)
        wanted = (iota((pair, mask_rows), 0) // piece) * (mask_rows // 2) + c
        pick = (iota((pair, mask_rows), 1) == wanted).astype(jnp.bfloat16)
        distance = squares + col_squares - 2.0 * cross
        value = jnp.exp(-(distance * row_sharp * col_sharp)) * quick(pick, col_mask)
        w_high[c], w_low[c] = split(value)
        part[0, c, :pair] = product(c, labels)
        sums = to_line(jnp.sum(value, axis=1, keepdims=True))
        part[0, c, pair:, :pair] = jnp.broadcast_to(sums, (AUX, pair))

    def send_part(step, other, depth):
        push(
            part.at[step, other, pl.ds(0, depth)], summed.at[step, z, pl.ds(0, depth)],
            sum_sem.at[step, z], (r, other),
        )

    if others_z:
        hand_on(others_z[0])
    arrived(row_emb.at[2 * z + 1 - core], row_sem.at[2 * z + 1 - core])
    block(z)
    for i, other in enumerate(others_z):
        if i + 1 < len(others_z):
            hand_on(others_z[i + 1])
        slot = 2 * other + 1 - core
        arrived(row_emb.at[slot], row_sem.at[slot])
        block(other)
        send_part(0, other, pair + AUX)

    kept = jnp.concatenate([first[2 * chip, :piece], first[2 * chip + 1, :piece]], axis=0)
    kept = 0.1 * kept
    scale = None
    for step in range(ITERS):
        if step > 0:
            labels = jnp.concatenate(split(later[step - 1].reshape(n_cols, half)), axis=1)
        if step < ITERS - 1:
            depth = pair + AUX if step == 0 else pair
            if step > 0:
                for other in reversed(others_z):
                    part[step, other, :pair] = product(other, labels)
                    send_part(step, other, depth)
                part[step, z, :pair] = product(z, labels)
            total = part[step, z, :depth]
            for other in others_z:
                arrived(summed.at[step, other, pl.ds(0, depth)], sum_sem.at[step, other])
                total = total + summed[step, other, :depth]
            if step == 0:
                scale = 0.9 / to_column(total[pair : pair + 1, :pair])
            later[step, chip] = total[:pair] * scale + kept
            for other in reversed(others_chip):
                push(
                    later.at[step, chip], later.at[step, chip], later_sem.at[step, chip],
                    (2 * other + core, z),
                )
            for other in others_chip:
                arrived(later.at[step, other], later_sem.at[step, other])
        else:
            for other in reversed(others_z):
                last_part[other] = product(other, labels).reshape(2, piece, half)
                for k in range(2):
                    push(last_part.at[other, k], last.at[z, core], last_sem.at[z, core], (2 * chip + k, other))
            last_part[z] = product(z, labels).reshape(2, piece, half)
            push(last_part.at[z, 1 - core], last.at[z, core], last_sem.at[z, core], (twin, z))
            last[z, core] = last_part[z, core]
            arrived(last.at[z, 1 - core], last_sem.at[z, 1 - core])
            for other in others_z:
                for k in range(2):
                    arrived(last.at[other, k], last_sem.at[other, k])
            total = jnp.sum(last[...], axis=0)
            own = jnp.where(core == 0, scale[:piece], scale[piece:])
            for k in range(2):
                out_ref[:, k * half : (k + 1) * half] = total[k] * own + 0.1 * send[k, :piece]
    for copy in sent:
        copy.wait_send()


def round_up(n, m):
    return (n + m - 1) // m * m


def local(chips, cols, embeddings, sharpness, soft_labels, seed_mask, tile_mask):
    piece, width = embeddings.shape
    half = soft_labels.shape[1] // 2
    rows = 2 * chips
    tile_rows, tiles = round_up(tile_mask.shape[0], 8), round_up(tile_mask.shape[1], 128)
    pair = 2 * piece
    sends = (
        2 * (cols - 1) + 2 * (chips - 1) + 2 + 1 + 2 * (cols - 1) + 1 + 2 * (chips - 1) + 1
        + (ITERS - 1) * (cols + chips - 2) + 2 * cols - 1
    )
    f32, bf16, dma = jnp.float32, jnp.bfloat16, pltpu.SemaphoreType.DMA
    vmem = pl.BlockSpec(memory_space=pltpu.VMEM)
    return pl.pallas_call(
        functools.partial(kernel, chips, cols),
        out_shape=jax.ShapeDtypeStruct(soft_labels.shape, f32),
        in_specs=[pl.BlockSpec(memory_space=pltpu.HBM)] * 5,
        out_specs=vmem,
        scratch_shapes=[
            pltpu.VMEM((2 * cols, piece, width), f32),
            pltpu.VMEM((rows, piece, width), f32),
            pltpu.VMEM((2 * cols, AUX, 128), f32),
            pltpu.VMEM((2, tile_rows, tiles), f32),
            pltpu.VMEM((rows, piece + AUX, half), f32),
            pltpu.VMEM((ITERS - 1, chips, pair, half), f32),
            pltpu.VMEM((ITERS - 1, cols, pair + AUX, half), f32),
            pltpu.VMEM((ITERS - 1, cols, pair + AUX, half), f32),
            pltpu.VMEM((cols, 2, piece, half), f32),
            pltpu.VMEM((cols, 2, piece, half), f32),
            pltpu.VMEM((cols, pair, rows * piece), bf16),
            pltpu.VMEM((cols, pair, rows * piece), bf16),
            pltpu.VMEM((rows * piece, width), bf16),
            pltpu.VMEM((rows * piece, width), bf16),
            pltpu.VMEM((2, piece + AUX, half), f32),
            pltpu.VMEM(soft_labels.shape, f32),
            pltpu.VMEM((1, piece), f32),
            pltpu.VMEM((1, piece), jnp.int32),
            pltpu.VMEM(tile_mask.shape, jnp.int32),
            dma((2 * cols,)),
            dma((rows,)),
            dma((2 * cols,)),
            dma(()),
            dma((rows,)),
            dma((ITERS - 1, chips)),
            dma((ITERS - 1, cols)),
            dma((cols, 2)),
            dma((sends,)),
            dma((6,)),
        ],
        compiler_params=pltpu.CompilerParams(
            collective_id=0, has_side_effects=True, vmem_limit_bytes=48 * 1024 * 1024
        ),
    )(embeddings, sharpness.reshape(1, piece), soft_labels, seed_mask.reshape(1, piece), tile_mask)


def solution(mesh):
    return jax.shard_map(
        functools.partial(local, mesh.shape["row"] // 2, mesh.shape["col"]),
        mesh=mesh,
        in_specs=(
            P(("row", "col"), None),
            P(("row", "col")),
            P(("row", "col"), None),
            P(("row", "col")),
            P("row", None),
        ),
        out_specs=P(("row", "col"), None),
        check_vma=False,
    )
```

```python
import functools

import jax
import jax.numpy as jnp
from jax import lax
from jax.experimental import pallas as pl
from jax.experimental.pallas import tpu as pltpu
from jax.sharding import PartitionSpec as P

ITERS = 3
MESH = pl.DeviceIdType.MESH
EXACT = lax.Precision.HIGHEST
AUX = 8


def dot(a, b, a_dim=1, b_dim=0):
    return lax.dot_general(
        a, b, (((a_dim,), (b_dim,)), ((), ())), precision=EXACT, preferred_element_type=jnp.float32
    )


def iota(shape, dim):
    return lax.broadcasted_iota(jnp.int32, shape, dim)


def to_column(line):
    n = line.shape[1]
    eye = iota((n, n), 0) == iota((n, n), 1)
    return jnp.sum(jnp.where(eye, jnp.broadcast_to(line, (n, n)), 0.0), axis=1, keepdims=True)


def to_line(column):
    n = column.shape[0]
    eye = iota((n, n), 0) == iota((n, n), 1)
    return jnp.sum(jnp.where(eye, jnp.broadcast_to(column, (n, n)), 0.0), axis=0, keepdims=True)


def split(value):
    high = value.astype(jnp.bfloat16)
    return high, (value - high.astype(jnp.float32)).astype(jnp.bfloat16)


def quick(a, b, b_dim=0):
    return lax.dot_general(a, b, (((1,), (b_dim,)), ((), ())), preferred_element_type=jnp.float32)


def by_distance(n):
    return sorted(range(1, n), key=lambda d: (min(d, n - d), d))


def kernel(
    chips, cols, emb_ref, sharp_ref, soft_ref, seed_ref, tile_ref, out_ref,
    row_emb, col_emb, row_aux, mask_buf, col_mask, first, tiles, later, part, summed, last_part, last,
    w_high, w_low, c_high, c_low, send, soft, sharp_in, seed_in, tile_in,
    row_sem, col_sem, aux_sem, tile_sem, first_sem, later_sem, sum_sem, last_sem, send_sem, load_sem,
):
    piece, width = emb_ref.shape
    half = soft_ref.shape[1] // 2
    rows = 2 * chips
    pair = 2 * piece
    r, z = lax.axis_index("row"), lax.axis_index("col")
    chip, core = r // 2, lax.rem(r, 2)
    twin = r + 1 - 2 * core

    others_z = [lax.rem(z + d, cols) for d in by_distance(cols)]
    others_chip = [lax.rem(chip + d, chips) for d in by_distance(chips)]
    peers = [(twin, z)]
    peers += [(2 * chip + k, other) for other in others_z for k in range(2)]
    peers += [(2 * other + k, z) for other in others_chip for k in range(2)]

    barrier = pltpu.get_barrier_semaphore()
    for peer in peers:
        pl.semaphore_signal(barrier, inc=1, device_id=peer, device_id_type=MESH)
    loads = []
    for src, dst in (
        (emb_ref, row_emb.at[z]), (emb_ref, col_emb.at[r]), (soft_ref, soft), (sharp_ref, sharp_in),
        (seed_ref, seed_in), (tile_ref, tile_in),
    ):
        loads.append(pltpu.make_async_copy(src, dst, load_sem.at[len(loads)]))
        loads[-1].start()
    sent = []

    def push(src, dst, recv, peer):
        copy = pltpu.make_async_remote_copy(
            src_ref=src, dst_ref=dst, send_sem=send_sem.at[len(sent)], recv_sem=recv,
            device_id=peer, device_id_type=MESH,
        )
        copy.start()
        sent.append(copy)

    def arrived(dst, recv):
        pltpu.make_async_remote_copy(
            src_ref=dst, dst_ref=dst, send_sem=send_sem.at[0], recv_sem=recv,
            device_id=(twin, z), device_id_type=MESH,
        ).wait_recv()

    for load in loads:
        load.wait()
    aux = jnp.concatenate([sharp_in[...], jnp.zeros((1, 128 - piece), jnp.float32)], axis=1)
    aux = jnp.broadcast_to(aux, (AUX, 128))
    row_aux[z] = aux
    seeded = to_column(seed_in[...].astype(jnp.float32)) * soft[...]
    for k in range(2):
        send[k, :piece] = seeded[:, k * half : (k + 1) * half]
        send[k, piece:, :128] = aux
    first[r] = send[core]
    pl.semaphore_wait(barrier, len(peers))

    for other in others_z:
        push(row_emb.at[z], row_emb.at[z], row_sem.at[z], (r, other))
    for other in others_chip:
        push(col_emb.at[r], col_emb.at[r], col_sem.at[r], (2 * other + core, z))
    push(col_emb.at[r], col_emb.at[r], col_sem.at[r], (twin, z))
    for other in others_chip:
        for k in range(2):
            push(send.at[k], first.at[r], first_sem.at[r], (2 * other + k, z))
    push(send.at[1 - core], first.at[r], first_sem.at[r], (twin, z))
    for other in others_z:
        push(row_aux.at[z], row_aux.at[z], aux_sem.at[z], (r, other))

    n_cols = rows * piece
    n_tiles = mask_buf.shape[1]
    mask_buf[...] = jnp.zeros(mask_buf.shape, jnp.float32)
    mask_buf[: tile_ref.shape[0], : tile_ref.shape[1]] = tile_in[...].astype(jnp.float32)
    wanted = (iota((n_tiles, n_cols), 1) // piece) * cols + z
    pick_cols = (iota((n_tiles, n_cols), 0) == wanted).astype(jnp.bfloat16)
    col_mask[...] = quick(mask_buf[...].astype(jnp.bfloat16), pick_cols)

    for other in others_chip:
        slot = 2 * other + core
        arrived(col_emb.at[slot], col_sem.at[slot])
        push(col_emb.at[slot], col_emb.at[slot], col_sem.at[slot], (twin, z))

    def take(slot):
        theirs = col_emb[slot]
        at = pl.ds(pl.multiple_of(slot * piece, piece), piece)
        c_high[at], c_low[at] = split(theirs)

    take(r)
    for other in others_chip:
        take(2 * other + core)

    arrived(first.at[twin], first_sem.at[twin])
    for other in others_chip:
        for k in range(2):
            arrived(first.at[2 * other + k], first_sem.at[2 * other + k])
    line = first[:, piece:, :128].reshape(rows * AUX, 128)[:, :piece]
    at = iota((piece, n_cols), 1)
    spread = dot(line, (iota((piece, n_cols), 0) == lax.rem(at, piece)).astype(jnp.float32))
    at = iota((rows * AUX, n_cols), 1)
    keep = iota((rows * AUX, n_cols), 0) == (at // piece) * AUX
    col_sharp = jnp.sum(jnp.where(keep, spread, 0.0), axis=0, keepdims=True)
    labels = jnp.concatenate(split(first[:, :piece].reshape(n_cols, half)), axis=1)

    arrived(col_emb.at[twin], col_sem.at[twin])
    take(twin)
    for other in others_chip:
        slot = 2 * other + 1 - core
        arrived(col_emb.at[slot], col_sem.at[slot])
        take(slot)
    theirs = col_emb[...].reshape(n_cols, width)
    col_squares = dot(jnp.ones((8, width), jnp.float32), theirs * theirs, 1, 1)[:1]

    def product(c, labels):
        wide = quick(w_high[c], labels)
        return wide[:, :half] + wide[:, half:] + quick(w_low[c], labels[:, :half])

    def block(c):
        ours = row_emb[c]
        both = jnp.concatenate(split(ours), axis=0)
        by_high, by_low = quick(both, c_high[...], 1), quick(both, c_low[...], 1)
        cross = by_high[:piece] + (by_high[piece:] + by_low[:piece] + by_low[piece:])
        squares = jnp.sum(ours * ours, axis=1, keepdims=True)
        row_sharp = to_column(row_aux[c][:1, :piece])
        distance = squares + col_squares - 2.0 * cross
        value = jnp.exp(-(distance * row_sharp * col_sharp)) * col_mask[pl.ds(c, 1)]
        tiles[c, core] = value
        push(tiles.at[c, core], tiles.at[c, core], tile_sem.at[c], (twin, z))

    def finish(c):
        arrived(tiles.at[c, 1 - core], tile_sem.at[c])
        value = tiles[c].reshape(pair, n_cols)
        w_high[c], w_low[c] = split(value)
        part[0, c, :pair] = product(c, labels)
        sums = to_line(jnp.sum(value, axis=1, keepdims=True))
        part[0, c, pair:, :pair] = jnp.broadcast_to(sums, (AUX, pair))

    def send_part(step, other, depth):
        push(
            part.at[step, other, pl.ds(0, depth)], summed.at[step, z, pl.ds(0, depth)],
            sum_sem.at[step, z], (r, other),
        )

    block(z)
    for i, other in enumerate(others_z):
        arrived(row_aux.at[other], aux_sem.at[other])
        arrived(row_emb.at[other], row_sem.at[other])
        block(other)
        before = others_z[i - 1] if i else z
        finish(before)
        if i:
            send_part(0, before, pair + AUX)
    if others_z:
        finish(others_z[-1])
        send_part(0, others_z[-1], pair + AUX)
    else:
        finish(z)

    kept = jnp.concatenate([first[2 * chip, :piece], first[2 * chip + 1, :piece]], axis=0)
    kept = 0.1 * kept
    scale = None
    for step in range(ITERS):
        if step > 0:
            labels = jnp.concatenate(split(later[step - 1].reshape(n_cols, half)), axis=1)
        if step < ITERS - 1:
            depth = pair + AUX if step == 0 else pair
            if step > 0:
                for other in reversed(others_z):
                    part[step, other, :pair] = product(other, labels)
                    send_part(step, other, depth)
                part[step, z, :pair] = product(z, labels)
            total = part[step, z, :depth]
            for other in others_z:
                arrived(summed.at[step, other, pl.ds(0, depth)], sum_sem.at[step, other])
                total = total + summed[step, other, :depth]
            if step == 0:
                scale = 0.9 / to_column(total[pair : pair + 1, :pair])
            later[step, chip] = total[:pair] * scale + kept
            for other in reversed(others_chip):
                push(
                    later.at[step, chip], later.at[step, chip], later_sem.at[step, chip],
                    (2 * other + core, z),
                )
            for other in others_chip:
                arrived(later.at[step, other], later_sem.at[step, other])
        else:
            for other in reversed(others_z):
                last_part[other] = product(other, labels).reshape(2, piece, half)
                for k in range(2):
                    push(last_part.at[other, k], last.at[z, core], last_sem.at[z, core], (2 * chip + k, other))
            last_part[z] = product(z, labels).reshape(2, piece, half)
            push(last_part.at[z, 1 - core], last.at[z, core], last_sem.at[z, core], (twin, z))
            last[z, core] = last_part[z, core]
            arrived(last.at[z, 1 - core], last_sem.at[z, 1 - core])
            for other in others_z:
                for k in range(2):
                    arrived(last.at[other, k], last_sem.at[other, k])
            total = jnp.sum(last[...], axis=0)
            own = jnp.where(core == 0, scale[:piece], scale[piece:])
            for k in range(2):
                out_ref[:, k * half : (k + 1) * half] = total[k] * own + 0.1 * send[k, :piece]
    for copy in sent:
        copy.wait_send()


def round_up(n, m):
    return (n + m - 1) // m * m


def local(chips, cols, embeddings, sharpness, soft_labels, seed_mask, tile_mask):
    piece, width = embeddings.shape
    half = soft_labels.shape[1] // 2
    rows = 2 * chips
    tile_rows, n_tiles = round_up(tile_mask.shape[0], 16), round_up(tile_mask.shape[1], 128)
    pair = 2 * piece
    sends = (
        (cols - 1) + (chips - 1) + 1 + 2 * (chips - 1) + 1 + (cols - 1) + (chips - 1) + cols
        + (ITERS - 1) * (cols + chips - 2) + 2 * cols - 1
    )
    f32, bf16, dma = jnp.float32, jnp.bfloat16, pltpu.SemaphoreType.DMA
    vmem = pl.BlockSpec(memory_space=pltpu.VMEM)
    return pl.pallas_call(
        functools.partial(kernel, chips, cols),
        out_shape=jax.ShapeDtypeStruct(soft_labels.shape, f32),
        in_specs=[pl.BlockSpec(memory_space=pltpu.HBM)] * 5,
        out_specs=vmem,
        scratch_shapes=[
            pltpu.VMEM((cols, piece, width), f32),
            pltpu.VMEM((rows, piece, width), f32),
            pltpu.VMEM((cols, AUX, 128), f32),
            pltpu.VMEM((tile_rows, n_tiles), f32),
            pltpu.VMEM((tile_rows, rows * piece), f32),
            pltpu.VMEM((rows, piece + AUX, half), f32),
            pltpu.VMEM((cols, 2, piece, rows * piece), f32),
            pltpu.VMEM((ITERS - 1, chips, pair, half), f32),
            pltpu.VMEM((ITERS - 1, cols, pair + AUX, half), f32),
            pltpu.VMEM((ITERS - 1, cols, pair + AUX, half), f32),
            pltpu.VMEM((cols, 2, piece, half), f32),
            pltpu.VMEM((cols, 2, piece, half), f32),
            pltpu.VMEM((cols, pair, rows * piece), bf16),
            pltpu.VMEM((cols, pair, rows * piece), bf16),
            pltpu.VMEM((rows * piece, width), bf16),
            pltpu.VMEM((rows * piece, width), bf16),
            pltpu.VMEM((2, piece + AUX, half), f32),
            pltpu.VMEM(soft_labels.shape, f32),
            pltpu.VMEM((1, piece), f32),
            pltpu.VMEM((1, piece), jnp.int32),
            pltpu.VMEM(tile_mask.shape, jnp.int32),
            dma((cols,)),
            dma((rows,)),
            dma((cols,)),
            dma((cols,)),
            dma((rows,)),
            dma((ITERS - 1, chips)),
            dma((ITERS - 1, cols)),
            dma((cols, 2)),
            dma((sends,)),
            dma((6,)),
        ],
        compiler_params=pltpu.CompilerParams(
            collective_id=0, has_side_effects=True, vmem_limit_bytes=60 * 1024 * 1024
        ),
    )(embeddings, sharpness.reshape(1, piece), soft_labels, seed_mask.reshape(1, piece), tile_mask)


def solution(mesh):
    return jax.shard_map(
        functools.partial(local, mesh.shape["row"] // 2, mesh.shape["col"]),
        mesh=mesh,
        in_specs=(
            P(("row", "col"), None),
            P(("row", "col")),
            P(("row", "col"), None),
            P(("row", "col")),
            P("row", None),
        ),
        out_specs=P(("row", "col"), None),
        check_vma=False,
    )
```

```python
import functools

import jax
import jax.numpy as jnp
from jax import lax
from jax.experimental import pallas as pl
from jax.experimental.pallas import tpu as pltpu
from jax.sharding import PartitionSpec as P

ITERS = 3
MESH = pl.DeviceIdType.MESH
EXACT = lax.Precision.HIGHEST
AUX = 8


def dot(a, b, a_dim=1, b_dim=0):
    return lax.dot_general(
        a, b, (((a_dim,), (b_dim,)), ((), ())), precision=EXACT, preferred_element_type=jnp.float32
    )


def iota(shape, dim):
    return lax.broadcasted_iota(jnp.int32, shape, dim)


def to_column(line):
    n = line.shape[1]
    eye = iota((n, n), 0) == iota((n, n), 1)
    return jnp.sum(jnp.where(eye, jnp.broadcast_to(line, (n, n)), 0.0), axis=1, keepdims=True)


def to_line(column):
    n = column.shape[0]
    eye = iota((n, n), 0) == iota((n, n), 1)
    return jnp.sum(jnp.where(eye, jnp.broadcast_to(column, (n, n)), 0.0), axis=0, keepdims=True)


def split(value):
    high = value.astype(jnp.bfloat16)
    return high, (value - high.astype(jnp.float32)).astype(jnp.bfloat16)


def quick(a, b, b_dim=0):
    return lax.dot_general(a, b, (((1,), (b_dim,)), ((), ())), preferred_element_type=jnp.float32)


def by_distance(n):
    return sorted(range(1, n), key=lambda d: (min(d, n - d), d))


def kernel(
    chips, cols, emb_ref, sharp_ref, soft_ref, seed_ref, tile_ref, out_ref,
    row_emb, col_buf, row_aux, mask_buf, col_mask, tiles, part, summed, new_labels, later,
    next_part, next_sum, last_labels, last_part, last,
    w_high, w_low, c_high, c_low, soft, sharp_in, seed_in, tile_in,
    row_sem, col_sem, aux_sem, tile_sem, later_sem, sum_sem, last_label_sem, next_sum_sem, last_sem,
    send_sem, load_sem,
):
    piece, width = emb_ref.shape
    n_labels = soft_ref.shape[1]
    half = n_labels // 2
    rows = 2 * chips
    pair = 2 * piece
    end = width + n_labels
    r, z = lax.axis_index("row"), lax.axis_index("col")
    chip, core = r // 2, lax.rem(r, 2)
    twin = r + 1 - 2 * core

    others_z = [lax.rem(z + d, cols) for d in by_distance(cols)]
    others_chip = [lax.rem(chip + d, chips) for d in by_distance(chips)]
    peers = [(twin, z)]
    peers += [(2 * chip + k, other) for other in others_z for k in range(2)]
    peers += [(2 * other + k, z) for other in others_chip for k in range(2)]

    barrier = pltpu.get_barrier_semaphore()
    for peer in peers:
        pl.semaphore_signal(barrier, inc=1, device_id=peer, device_id_type=MESH)
    loads = []
    for src, dst in (
        (emb_ref, row_emb.at[z]), (emb_ref, col_buf.at[r, :, pl.ds(0, width)]), (soft_ref, soft),
        (sharp_ref, sharp_in), (seed_ref, seed_in), (tile_ref, tile_in),
    ):
        loads.append(pltpu.make_async_copy(src, dst, load_sem.at[len(loads)]))
        loads[-1].start()
    sent = []

    def push(src, dst, recv, peer):
        copy = pltpu.make_async_remote_copy(
            src_ref=src, dst_ref=dst, send_sem=send_sem.at[len(sent)], recv_sem=recv,
            device_id=peer, device_id_type=MESH,
        )
        copy.start()
        sent.append(copy)

    def arrived(dst, recv):
        pltpu.make_async_remote_copy(
            src_ref=dst, dst_ref=dst, send_sem=send_sem.at[0], recv_sem=recv,
            device_id=(twin, z), device_id_type=MESH,
        ).wait_recv()

    for load in loads:
        load.wait()
    aux = jnp.concatenate([sharp_in[...], jnp.zeros((1, 128 - piece), jnp.float32)], axis=1)
    row_aux[z] = jnp.broadcast_to(aux, (AUX, 128))
    col_buf[r, :, end:] = jnp.broadcast_to(aux, (piece, 128))
    seeded = to_column(seed_in[...].astype(jnp.float32)) * soft[...]
    col_buf[r, :, width:end] = seeded
    pl.semaphore_wait(barrier, len(peers))

    for other in others_z:
        push(row_emb.at[z], row_emb.at[z], row_sem.at[z], (r, other))
    for other in others_chip:
        push(col_buf.at[r], col_buf.at[r], col_sem.at[r], (2 * other + core, z))
    push(col_buf.at[r], col_buf.at[r], col_sem.at[r], (twin, z))
    for other in others_z:
        push(row_aux.at[z], row_aux.at[z], aux_sem.at[z], (r, other))

    n_cols = rows * piece
    n_tiles = mask_buf.shape[1]
    mask_buf[...] = jnp.zeros(mask_buf.shape, jnp.float32)
    mask_buf[: tile_ref.shape[0], : tile_ref.shape[1]] = tile_in[...].astype(jnp.float32)
    wanted = (iota((n_tiles, n_cols), 1) // piece) * cols + z
    pick_cols = (iota((n_tiles, n_cols), 0) == wanted).astype(jnp.bfloat16)
    col_mask[...] = quick(mask_buf[...].astype(jnp.bfloat16), pick_cols)

    def take(slot):
        at = pl.ds(pl.multiple_of(slot * piece, piece), piece)
        c_high[at], c_low[at] = split(col_buf[slot, :, :width])

    take(r)
    for other in others_chip:
        slot = 2 * other + core
        arrived(col_buf.at[slot], col_sem.at[slot])
        push(col_buf.at[slot], col_buf.at[slot], col_sem.at[slot], (twin, z))
    for other in others_chip:
        take(2 * other + core)
    arrived(col_buf.at[twin], col_sem.at[twin])
    take(twin)
    for other in others_chip:
        slot = 2 * other + 1 - core
        arrived(col_buf.at[slot], col_sem.at[slot])
        take(slot)
    theirs = col_buf[:, :, :width].reshape(n_cols, width)
    col_squares = dot(jnp.ones((8, width), jnp.float32), theirs * theirs, 1, 1)[:1]
    line = col_buf[:, :AUX, end:].reshape(rows * AUX, 128)[:, :piece]
    at = iota((piece, n_cols), 1)
    spread = dot(line, (iota((piece, n_cols), 0) == lax.rem(at, piece)).astype(jnp.float32))
    at = iota((rows * AUX, n_cols), 1)
    keep = iota((rows * AUX, n_cols), 0) == (at // piece) * AUX
    col_sharp = jnp.sum(jnp.where(keep, spread, 0.0), axis=0, keepdims=True)
    labels = jnp.concatenate(split(col_buf[:, :, width:end].reshape(n_cols, n_labels)), axis=1)

    def block(c):
        ours = row_emb[c]
        both = jnp.concatenate(split(ours), axis=0)
        by_high, by_low = quick(both, c_high[...], 1), quick(both, c_low[...], 1)
        cross = by_high[:piece] + (by_high[piece:] + by_low[:piece] + by_low[piece:])
        squares = jnp.sum(ours * ours, axis=1, keepdims=True)
        row_sharp = to_column(row_aux[c][:1, :piece])
        distance = squares + col_squares - 2.0 * cross
        value = jnp.exp(-(distance * row_sharp * col_sharp)) * col_mask[pl.ds(c, 1)]
        tiles[c, core] = value
        wide = quick(jnp.concatenate(split(value), axis=0), labels)
        low = wide[piece:, :n_labels] + wide[piece:, n_labels:] + wide[:piece, n_labels:]
        part[c, :piece] = wide[:piece, :n_labels] + low
        sums = to_line(jnp.sum(value, axis=1, keepdims=True))
        part[c, piece:, :piece] = jnp.broadcast_to(sums, (AUX, piece))

    block(z)
    for other in others_z:
        arrived(row_aux.at[other], aux_sem.at[other])
        arrived(row_emb.at[other], row_sem.at[other])
        block(other)
        push(part.at[other], summed.at[z], sum_sem.at[z], (r, other))
    for other in [z] + others_z:
        push(tiles.at[other, core], tiles.at[other, core], tile_sem.at[other], (twin, z))

    total = part[z]
    for other in others_z:
        arrived(summed.at[other], sum_sem.at[other])
        total = total + summed[other]
    degree = total[piece : piece + 1, :piece]
    own_scale = 0.9 / to_column(degree)
    own_kept = 0.1 * col_buf[r, :, width:end]
    value = total[:piece] * own_scale + own_kept
    for k in range(2):
        new_labels[k, :piece] = value[:, k * half : (k + 1) * half]
        new_labels[k, piece:, :piece] = jnp.broadcast_to(degree, (AUX, piece))
    for other in others_chip:
        for k in range(2):
            push(new_labels.at[k], later.at[r], later_sem.at[r], (2 * other + k, z))
    push(new_labels.at[1 - core], later.at[r], later_sem.at[r], (twin, z))
    later[r] = new_labels[core]

    for c in [z] + others_z:
        arrived(tiles.at[c, 1 - core], tile_sem.at[c])
        w_high[c], w_low[c] = split(tiles[c].reshape(pair, n_cols))

    def product(c, labels):
        wide = quick(w_high[c], labels)
        return wide[:, :half] + wide[:, half:] + quick(w_low[c], labels[:, :half])

    arrived(later.at[twin], later_sem.at[twin])
    for other in others_chip:
        for k in range(2):
            slot = 2 * other + k
            arrived(later.at[slot], later_sem.at[slot])

    pieces = [2 * chip, 2 * chip + 1]
    kept = jnp.concatenate([col_buf[p, :, width:end] for p in pieces], axis=0)
    kept = 0.1 * jnp.where(core == 0, kept[:, :half], kept[:, half:])
    scale = jnp.concatenate([0.9 / to_column(later[p, piece : piece + 1, :piece]) for p in pieces], axis=0)
    labels = later[:, :piece].reshape(n_cols, half)
    for step in range(ITERS - 2):
        labels = jnp.concatenate(split(labels), axis=1)
        for other in reversed(others_z):
            next_part[step, other] = product(other, labels)
            push(
                next_part.at[step, other], next_sum.at[step, z], next_sum_sem.at[step, z], (r, other)
            )
        total = product(z, labels)
        for other in others_z:
            arrived(next_sum.at[step, other], next_sum_sem.at[step, other])
            total = total + next_sum[step, other]
        last_labels[step, chip] = total * scale + kept
        for other in reversed(others_chip):
            push(
                last_labels.at[step, chip], last_labels.at[step, chip], last_label_sem.at[step, chip],
                (2 * other + core, z),
            )
        for other in others_chip:
            arrived(last_labels.at[step, other], last_label_sem.at[step, other])
        labels = last_labels[step].reshape(n_cols, half)

    labels = jnp.concatenate(split(labels), axis=1)
    for other in reversed(others_z):
        last_part[other] = product(other, labels).reshape(2, piece, half)
        for k in range(2):
            push(last_part.at[other, k], last.at[z, core], last_sem.at[z, core], (2 * chip + k, other))
    last_part[z] = product(z, labels).reshape(2, piece, half)
    push(last_part.at[z, 1 - core], last.at[z, core], last_sem.at[z, core], (twin, z))
    last[z, core] = last_part[z, core]
    arrived(last.at[z, 1 - core], last_sem.at[z, 1 - core])
    for other in others_z:
        for k in range(2):
            arrived(last.at[other, k], last_sem.at[other, k])
    total = jnp.sum(last[...], axis=0)
    for k in range(2):
        at = slice(k * half, (k + 1) * half)
        out_ref[:, at] = total[k] * own_scale + own_kept[:, at]
    for copy in sent:
        copy.wait_send()


def round_up(n, m):
    return (n + m - 1) // m * m


def local(chips, cols, embeddings, sharpness, soft_labels, seed_mask, tile_mask):
    piece, width = embeddings.shape
    half = soft_labels.shape[1] // 2
    rows = 2 * chips
    tile_rows, n_tiles = round_up(tile_mask.shape[0], 16), round_up(tile_mask.shape[1], 128)
    pair = 2 * piece
    n_cols = rows * piece
    middle = ITERS - 2
    sends = (
        2 * (cols - 1) + 2 * (chips - 1) + 1 + (cols - 1) + cols + 2 * (chips - 1) + 1
        + middle * (cols + chips - 2) + 2 * cols - 1
    )
    f32, bf16, dma = jnp.float32, jnp.bfloat16, pltpu.SemaphoreType.DMA
    vmem = pl.BlockSpec(memory_space=pltpu.VMEM)
    return pl.pallas_call(
        functools.partial(kernel, chips, cols),
        out_shape=jax.ShapeDtypeStruct(soft_labels.shape, f32),
        in_specs=[pl.BlockSpec(memory_space=pltpu.HBM)] * 5,
        out_specs=vmem,
        scratch_shapes=[
            pltpu.VMEM((cols, piece, width), f32),
            pltpu.VMEM((rows, piece, width + 2 * half + 128), f32),
            pltpu.VMEM((cols, AUX, 128), f32),
            pltpu.VMEM((tile_rows, n_tiles), f32),
            pltpu.VMEM((tile_rows, n_cols), f32),
            pltpu.VMEM((cols, 2, piece, n_cols), f32),
            pltpu.VMEM((cols, piece + AUX, 2 * half), f32),
            pltpu.VMEM((cols, piece + AUX, 2 * half), f32),
            pltpu.VMEM((2, piece + AUX, half), f32),
            pltpu.VMEM((rows, piece + AUX, half), f32),
            pltpu.VMEM((middle, cols, pair, half), f32),
            pltpu.VMEM((middle, cols, pair, half), f32),
            pltpu.VMEM((middle, chips, pair, half), f32),
            pltpu.VMEM((cols, 2, piece, half), f32),
            pltpu.VMEM((cols, 2, piece, half), f32),
            pltpu.VMEM((cols, pair, n_cols), bf16),
            pltpu.VMEM((cols, pair, n_cols), bf16),
            pltpu.VMEM((n_cols, width), bf16),
            pltpu.VMEM((n_cols, width), bf16),
            pltpu.VMEM(soft_labels.shape, f32),
            pltpu.VMEM((1, piece), f32),
            pltpu.VMEM((1, piece), jnp.int32),
            pltpu.VMEM(tile_mask.shape, jnp.int32),
            dma((cols,)),
            dma((rows,)),
            dma((cols,)),
            dma((cols,)),
            dma((rows,)),
            dma((cols,)),
            dma((middle, chips)),
            dma((middle, cols)),
            dma((cols, 2)),
            dma((sends,)),
            dma((6,)),
        ],
        compiler_params=pltpu.CompilerParams(
            collective_id=0, has_side_effects=True, vmem_limit_bytes=60 * 1024 * 1024
        ),
    )(embeddings, sharpness.reshape(1, piece), soft_labels, seed_mask.reshape(1, piece), tile_mask)


def solution(mesh):
    return jax.shard_map(
        functools.partial(local, mesh.shape["row"] // 2, mesh.shape["col"]),
        mesh=mesh,
        in_specs=(
            P(("row", "col"), None),
            P(("row", "col")),
            P(("row", "col"), None),
            P(("row", "col")),
            P("row", None),
        ),
        out_specs=P(("row", "col"), None),
        check_vma=False,
    )
```

```python
import functools

import jax
import jax.numpy as jnp
from jax import lax
from jax.experimental import pallas as pl
from jax.experimental.pallas import tpu as pltpu
from jax.sharding import PartitionSpec as P

ITERS = 3
MESH = pl.DeviceIdType.MESH
EXACT = lax.Precision.HIGHEST
AUX = 8


def dot(a, b, a_dim=1, b_dim=0):
    return lax.dot_general(
        a, b, (((a_dim,), (b_dim,)), ((), ())), precision=EXACT, preferred_element_type=jnp.float32
    )


def iota(shape, dim):
    return lax.broadcasted_iota(jnp.int32, shape, dim)


def to_column(line):
    n = line.shape[1]
    eye = iota((n, n), 0) == iota((n, n), 1)
    return jnp.sum(jnp.where(eye, jnp.broadcast_to(line, (n, n)), 0.0), axis=1, keepdims=True)


def to_line(column):
    n = column.shape[0]
    eye = iota((n, n), 0) == iota((n, n), 1)
    return jnp.sum(jnp.where(eye, jnp.broadcast_to(column, (n, n)), 0.0), axis=0, keepdims=True)


def split(value):
    high = value.astype(jnp.bfloat16)
    return high, (value - high.astype(jnp.float32)).astype(jnp.bfloat16)


def quick(a, b, b_dim=0):
    return lax.dot_general(a, b, (((1,), (b_dim,)), ((), ())), preferred_element_type=jnp.float32)


def by_distance(n):
    return sorted(range(1, n), key=lambda d: (min(d, n - d), d))


def kernel(
    chips, cols, emb_ref, sharp_ref, soft_ref, seed_ref, tile_ref, out_ref,
    row_emb, col_emb, row_aux, mask_buf, col_mask, first, tiles, later, part, summed, last_part, last,
    w_high, w_low, c_high, c_low, send, soft, sharp_in, seed_in, tile_in,
    row_sem, col_sem, aux_sem, tile_sem, first_sem, later_sem, sum_sem, last_sem, send_sem, load_sem,
):
    piece, width = emb_ref.shape
    half = soft_ref.shape[1] // 2
    rows = 2 * chips
    pair = 2 * piece
    r, z = lax.axis_index("row"), lax.axis_index("col")
    chip, core = r // 2, lax.rem(r, 2)
    twin = r + 1 - 2 * core

    others_z = [lax.rem(z + d, cols) for d in by_distance(cols)]
    others_chip = [lax.rem(chip + d, chips) for d in by_distance(chips)]
    peers = [(twin, z)]
    peers += [(2 * chip + k, other) for other in others_z for k in range(2)]
    peers += [(2 * other + k, z) for other in others_chip for k in range(2)]

    barrier = pltpu.get_barrier_semaphore()
    for peer in peers:
        pl.semaphore_signal(barrier, inc=1, device_id=peer, device_id_type=MESH)
    loads = []
    for src, dst in (
        (emb_ref, row_emb.at[z]), (emb_ref, col_emb.at[r]), (soft_ref, soft), (sharp_ref, sharp_in),
        (seed_ref, seed_in), (tile_ref, tile_in),
    ):
        loads.append(pltpu.make_async_copy(src, dst, load_sem.at[len(loads)]))
        loads[-1].start()
    sent = []

    def push(src, dst, recv, peer):
        copy = pltpu.make_async_remote_copy(
            src_ref=src, dst_ref=dst, send_sem=send_sem.at[len(sent)], recv_sem=recv,
            device_id=peer, device_id_type=MESH,
        )
        copy.start()
        sent.append(copy)

    def arrived(dst, recv):
        pltpu.make_async_remote_copy(
            src_ref=dst, dst_ref=dst, send_sem=send_sem.at[0], recv_sem=recv,
            device_id=(twin, z), device_id_type=MESH,
        ).wait_recv()

    for load in loads:
        load.wait()
    held = row_emb[z]
    norms = to_line(jnp.sum(held * held, axis=1, keepdims=True))
    lines = jnp.where(iota((AUX, piece), 0) == 0, sharp_in[...], norms)
    aux = jnp.concatenate([lines, jnp.zeros((AUX, 128 - piece), jnp.float32)], axis=1)
    row_aux[z] = aux
    seeded = to_column(seed_in[...].astype(jnp.float32)) * soft[...]
    for k in range(2):
        send[k, :piece] = seeded[:, k * half : (k + 1) * half]
        send[k, piece:, :128] = aux
    first[r] = send[core]
    pl.semaphore_wait(barrier, len(peers))

    for other in reversed(others_chip):
        push(col_emb.at[r], col_emb.at[r], col_sem.at[r], (2 * other + core, z))
    push(col_emb.at[r], col_emb.at[r], col_sem.at[r], (twin, z))
    for other in others_z:
        push(row_emb.at[z], row_emb.at[z], row_sem.at[z], (r, other))
    for other in others_chip:
        for k in range(2):
            push(send.at[k], first.at[r], first_sem.at[r], (2 * other + k, z))
    push(send.at[1 - core], first.at[r], first_sem.at[r], (twin, z))
    for other in others_z:
        push(row_aux.at[z], row_aux.at[z], aux_sem.at[z], (r, other))

    n_cols = rows * piece
    n_tiles = mask_buf.shape[1]
    mask_buf[...] = jnp.zeros(mask_buf.shape, jnp.float32)
    mask_buf[: tile_ref.shape[0], : tile_ref.shape[1]] = tile_in[...].astype(jnp.float32)
    wanted = (iota((n_tiles, n_cols), 1) // piece) * cols + z
    pick_cols = (iota((n_tiles, n_cols), 0) == wanted).astype(jnp.bfloat16)
    col_mask[...] = quick(mask_buf[...].astype(jnp.bfloat16), pick_cols)

    for other in others_chip:
        slot = 2 * other + core
        arrived(col_emb.at[slot], col_sem.at[slot])
        push(col_emb.at[slot], col_emb.at[slot], col_sem.at[slot], (twin, z))

    def take(slot):
        theirs = col_emb[slot]
        at = pl.ds(pl.multiple_of(slot * piece, piece), piece)
        c_high[at], c_low[at] = split(theirs)

    take(r)
    for other in others_chip:
        take(2 * other + core)

    arrived(first.at[twin], first_sem.at[twin])
    for other in others_chip:
        for k in range(2):
            arrived(first.at[2 * other + k], first_sem.at[2 * other + k])
    line = first[:, piece:, :128].reshape(rows * AUX, 128)[:, :piece]
    at = iota((piece, n_cols), 1)
    spread = dot(line, (iota((piece, n_cols), 0) == lax.rem(at, piece)).astype(jnp.float32))
    at = iota((rows * AUX, n_cols), 1)
    keep = iota((rows * AUX, n_cols), 0) == (at // piece) * AUX
    col_sharp = jnp.sum(jnp.where(keep, spread, 0.0), axis=0, keepdims=True)
    keep = iota((rows * AUX, n_cols), 0) == (at // piece) * AUX + 1
    col_squares = jnp.sum(jnp.where(keep, spread, 0.0), axis=0, keepdims=True)
    labels = jnp.concatenate(split(first[:, :piece].reshape(n_cols, half)), axis=1)

    arrived(col_emb.at[twin], col_sem.at[twin])
    take(twin)
    for other in others_chip:
        slot = 2 * other + 1 - core
        arrived(col_emb.at[slot], col_sem.at[slot])
        take(slot)

    def product(c, labels):
        wide = quick(w_high[c], labels)
        return wide[:, :half] + wide[:, half:] + quick(w_low[c], labels[:, :half])

    def block(c):
        ours = row_emb[c]
        both = jnp.concatenate(split(ours), axis=0)
        by_high, by_low = quick(both, c_high[...], 1), quick(both, c_low[...], 1)
        cross = by_high[:piece] + (by_high[piece:] + by_low[:piece] + by_low[piece:])
        squares = to_column(row_aux[c][1:2, :piece])
        row_sharp = to_column(row_aux[c][:1, :piece])
        distance = squares + col_squares - 2.0 * cross
        value = jnp.exp(-(distance * row_sharp * col_sharp)) * col_mask[pl.ds(c, 1)]
        tiles[c, core] = value
        push(tiles.at[c, core], tiles.at[c, core], tile_sem.at[c], (twin, z))

    def finish(c):
        arrived(tiles.at[c, 1 - core], tile_sem.at[c])
        value = tiles[c].reshape(pair, n_cols)
        w_high[c], w_low[c] = split(value)
        part[0, c, :pair] = product(c, labels)
        sums = to_line(jnp.sum(value, axis=1, keepdims=True))
        part[0, c, pair:, :pair] = jnp.broadcast_to(sums, (AUX, pair))

    def send_part(step, other, depth):
        push(
            part.at[step, other, pl.ds(0, depth)], summed.at[step, z, pl.ds(0, depth)],
            sum_sem.at[step, z], (r, other),
        )

    block(z)
    for i, other in enumerate(others_z):
        arrived(row_aux.at[other], aux_sem.at[other])
        arrived(row_emb.at[other], row_sem.at[other])
        block(other)
        before = others_z[i - 1] if i else z
        finish(before)
        if i:
            send_part(0, before, pair + AUX)
    if others_z:
        finish(others_z[-1])
        send_part(0, others_z[-1], pair + AUX)
    else:
        finish(z)

    kept = jnp.concatenate([first[2 * chip, :piece], first[2 * chip + 1, :piece]], axis=0)
    kept = 0.1 * kept
    scale = None
    for step in range(ITERS):
        if step > 0:
            labels = jnp.concatenate(split(later[step - 1].reshape(n_cols, half)), axis=1)
        if step < ITERS - 1:
            depth = pair + AUX if step == 0 else pair
            if step > 0:
                for other in reversed(others_z):
                    part[step, other, :pair] = product(other, labels)
                    send_part(step, other, depth)
                part[step, z, :pair] = product(z, labels)
            total = part[step, z, :depth]
            for other in others_z:
                arrived(summed.at[step, other, pl.ds(0, depth)], sum_sem.at[step, other])
                total = total + summed[step, other, :depth]
            if step == 0:
                scale = 0.9 / to_column(total[pair : pair + 1, :pair])
            later[step, chip] = total[:pair] * scale + kept
            for other in reversed(others_chip):
                push(
                    later.at[step, chip], later.at[step, chip], later_sem.at[step, chip],
                    (2 * other + core, z),
                )
            for other in others_chip:
                arrived(later.at[step, other], later_sem.at[step, other])
        else:
            for other in reversed(others_z):
                last_part[other] = product(other, labels).reshape(2, piece, half)
                for k in range(2):
                    push(last_part.at[other, k], last.at[z, core], last_sem.at[z, core], (2 * chip + k, other))
            last_part[z] = product(z, labels).reshape(2, piece, half)
            push(last_part.at[z, 1 - core], last.at[z, core], last_sem.at[z, core], (twin, z))
            last[z, core] = last_part[z, core]
            arrived(last.at[z, 1 - core], last_sem.at[z, 1 - core])
            for other in others_z:
                for k in range(2):
                    arrived(last.at[other, k], last_sem.at[other, k])
            total = jnp.sum(last[...], axis=0)
            own = jnp.where(core == 0, scale[:piece], scale[piece:])
            for k in range(2):
                out_ref[:, k * half : (k + 1) * half] = total[k] * own + 0.1 * send[k, :piece]
    for copy in sent:
        copy.wait_send()


def round_up(n, m):
    return (n + m - 1) // m * m


def local(chips, cols, embeddings, sharpness, soft_labels, seed_mask, tile_mask):
    piece, width = embeddings.shape
    half = soft_labels.shape[1] // 2
    rows = 2 * chips
    tile_rows, n_tiles = round_up(tile_mask.shape[0], 16), round_up(tile_mask.shape[1], 128)
    pair = 2 * piece
    sends = (
        (cols - 1) + (chips - 1) + 1 + 2 * (chips - 1) + 1 + (cols - 1) + (chips - 1) + cols
        + (ITERS - 1) * (cols + chips - 2) + 2 * cols - 1
    )
    f32, bf16, dma = jnp.float32, jnp.bfloat16, pltpu.SemaphoreType.DMA
    vmem = pl.BlockSpec(memory_space=pltpu.VMEM)
    return pl.pallas_call(
        functools.partial(kernel, chips, cols),
        out_shape=jax.ShapeDtypeStruct(soft_labels.shape, f32),
        in_specs=[pl.BlockSpec(memory_space=pltpu.HBM)] * 5,
        out_specs=vmem,
        scratch_shapes=[
            pltpu.VMEM((cols, piece, width), f32),
            pltpu.VMEM((rows, piece, width), f32),
            pltpu.VMEM((cols, AUX, 128), f32),
            pltpu.VMEM((tile_rows, n_tiles), f32),
            pltpu.VMEM((tile_rows, rows * piece), f32),
            pltpu.VMEM((rows, piece + AUX, half), f32),
            pltpu.VMEM((cols, 2, piece, rows * piece), f32),
            pltpu.VMEM((ITERS - 1, chips, pair, half), f32),
            pltpu.VMEM((ITERS - 1, cols, pair + AUX, half), f32),
            pltpu.VMEM((ITERS - 1, cols, pair + AUX, half), f32),
            pltpu.VMEM((cols, 2, piece, half), f32),
            pltpu.VMEM((cols, 2, piece, half), f32),
            pltpu.VMEM((cols, pair, rows * piece), bf16),
            pltpu.VMEM((cols, pair, rows * piece), bf16),
            pltpu.VMEM((rows * piece, width), bf16),
            pltpu.VMEM((rows * piece, width), bf16),
            pltpu.VMEM((2, piece + AUX, half), f32),
            pltpu.VMEM(soft_labels.shape, f32),
            pltpu.VMEM((1, piece), f32),
            pltpu.VMEM((1, piece), jnp.int32),
            pltpu.VMEM(tile_mask.shape, jnp.int32),
            dma((cols,)),
            dma((rows,)),
            dma((cols,)),
            dma((cols,)),
            dma((rows,)),
            dma((ITERS - 1, chips)),
            dma((ITERS - 1, cols)),
            dma((cols, 2)),
            dma((sends,)),
            dma((6,)),
        ],
        compiler_params=pltpu.CompilerParams(
            collective_id=0, has_side_effects=True, vmem_limit_bytes=60 * 1024 * 1024
        ),
    )(embeddings, sharpness.reshape(1, piece), soft_labels, seed_mask.reshape(1, piece), tile_mask)


def solution(mesh):
    return jax.shard_map(
        functools.partial(local, mesh.shape["row"] // 2, mesh.shape["col"]),
        mesh=mesh,
        in_specs=(
            P(("row", "col"), None),
            P(("row", "col")),
            P(("row", "col"), None),
            P(("row", "col")),
            P("row", None),
        ),
        out_specs=P(("row", "col"), None),
        check_vma=False,
    )
```

```python
import functools

import jax
import jax.numpy as jnp
from jax import lax
from jax.experimental import pallas as pl
from jax.experimental.pallas import tpu as pltpu
from jax.sharding import PartitionSpec as P

ITERS = 3
MESH = pl.DeviceIdType.MESH
EXACT = lax.Precision.HIGHEST
AUX = 8


def dot(a, b, a_dim=1, b_dim=0):
    return lax.dot_general(
        a, b, (((a_dim,), (b_dim,)), ((), ())), precision=EXACT, preferred_element_type=jnp.float32
    )


def iota(shape, dim):
    return lax.broadcasted_iota(jnp.int32, shape, dim)


def to_column(line):
    n = line.shape[1]
    eye = iota((n, n), 0) == iota((n, n), 1)
    return jnp.sum(jnp.where(eye, jnp.broadcast_to(line, (n, n)), 0.0), axis=1, keepdims=True)


def to_line(column):
    n = column.shape[0]
    eye = iota((n, n), 0) == iota((n, n), 1)
    return jnp.sum(jnp.where(eye, jnp.broadcast_to(column, (n, n)), 0.0), axis=0, keepdims=True)


def split(value):
    high = value.astype(jnp.bfloat16)
    return high, (value - high.astype(jnp.float32)).astype(jnp.bfloat16)


def quick(a, b, b_dim=0):
    return lax.dot_general(a, b, (((1,), (b_dim,)), ((), ())), preferred_element_type=jnp.float32)


def by_distance(n):
    return sorted(range(1, n), key=lambda d: (min(d, n - d), d))


def kernel(
    chips, cols, emb_ref, sharp_ref, soft_ref, seed_ref, tile_ref, out_ref,
    row_emb, col_emb, row_aux, mask_buf, col_mask, first, tiles, later, part, summed, last_part, last,
    w_high, w_low, c_high, c_low, send, soft, sharp_in, seed_in, tile_in,
    row_sem, col_sem, aux_sem, tile_sem, first_sem, later_sem, sum_sem, last_sem, send_sem, load_sem,
):
    piece, width = emb_ref.shape
    half = soft_ref.shape[1] // 2
    rows = 2 * chips
    pair = 2 * piece
    r, z = lax.axis_index("row"), lax.axis_index("col")
    chip, core = r // 2, lax.rem(r, 2)
    twin = r + 1 - 2 * core

    others_z = [lax.rem(z + d, cols) for d in by_distance(cols)]
    others_chip = [lax.rem(chip + d, chips) for d in by_distance(chips)]
    peers = [(twin, z)]
    peers += [(2 * chip + k, other) for other in others_z for k in range(2)]
    peers += [(2 * other + k, z) for other in others_chip for k in range(2)]

    barrier = pltpu.get_barrier_semaphore()
    for peer in peers:
        pl.semaphore_signal(barrier, inc=1, device_id=peer, device_id_type=MESH)
    loads = []
    for src, dst in (
        (emb_ref, row_emb.at[z]), (emb_ref, col_emb.at[r]), (soft_ref, soft), (sharp_ref, sharp_in),
        (seed_ref, seed_in), (tile_ref, tile_in),
    ):
        loads.append(pltpu.make_async_copy(src, dst, load_sem.at[len(loads)]))
        loads[-1].start()
    sent = []

    def push(src, dst, recv, peer):
        copy = pltpu.make_async_remote_copy(
            src_ref=src, dst_ref=dst, send_sem=send_sem.at[len(sent)], recv_sem=recv,
            device_id=peer, device_id_type=MESH,
        )
        copy.start()
        sent.append(copy)

    def arrived(dst, recv):
        pltpu.make_async_remote_copy(
            src_ref=dst, dst_ref=dst, send_sem=send_sem.at[0], recv_sem=recv,
            device_id=(twin, z), device_id_type=MESH,
        ).wait_recv()

    for load in loads:
        load.wait()
    held = row_emb[z]
    norms = to_line(jnp.sum(held * held, axis=1, keepdims=True))
    lines = jnp.where(iota((AUX, piece), 0) == 0, sharp_in[...], norms)
    aux = jnp.concatenate([lines, jnp.zeros((AUX, 128 - piece), jnp.float32)], axis=1)
    row_aux[z] = aux
    seeded = to_column(seed_in[...].astype(jnp.float32)) * soft[...]
    for k in range(2):
        send[k, :piece] = seeded[:, k * half : (k + 1) * half]
        send[k, piece:, :128] = aux
    first[r] = send[core]
    pl.semaphore_wait(barrier, len(peers))

    for other in reversed(others_chip):
        push(col_emb.at[r], col_emb.at[r], col_sem.at[r], (2 * other + core, z))
    push(col_emb.at[r], col_emb.at[r], col_sem.at[r], (twin, z))
    for other in others_z:
        push(row_emb.at[z], row_emb.at[z], row_sem.at[z], (r, other))
    for other in others_chip:
        for k in range(2):
            push(send.at[k], first.at[r], first_sem.at[r], (2 * other + k, z))
    push(send.at[1 - core], first.at[r], first_sem.at[r], (twin, z))
    for other in others_z:
        push(row_aux.at[z], row_aux.at[z], aux_sem.at[z], (r, other))

    n_cols = rows * piece
    n_tiles = mask_buf.shape[1]
    mask_buf[...] = jnp.zeros(mask_buf.shape, jnp.float32)
    mask_buf[: tile_ref.shape[0], : tile_ref.shape[1]] = tile_in[...].astype(jnp.float32)
    wanted = (iota((n_tiles, n_cols), 1) // piece) * cols + z
    pick_cols = (iota((n_tiles, n_cols), 0) == wanted).astype(jnp.bfloat16)
    col_mask[...] = quick(mask_buf[...].astype(jnp.bfloat16), pick_cols)

    for other in others_chip:
        slot = 2 * other + core
        arrived(col_emb.at[slot], col_sem.at[slot])
        push(col_emb.at[slot], col_emb.at[slot], col_sem.at[slot], (twin, z))

    def take(slot):
        theirs = col_emb[slot]
        at = pl.ds(pl.multiple_of(slot * piece, piece), piece)
        c_high[at], c_low[at] = split(theirs)

    take(r)
    for other in others_chip:
        take(2 * other + core)

    arrived(first.at[twin], first_sem.at[twin])
    for other in others_chip:
        for k in range(2):
            arrived(first.at[2 * other + k], first_sem.at[2 * other + k])
    line = first[:, piece:, :128].reshape(rows * AUX, 128)[:, :piece]
    at = iota((piece, n_cols), 1)
    spread = dot(line, (iota((piece, n_cols), 0) == lax.rem(at, piece)).astype(jnp.float32))
    at = iota((rows * AUX, n_cols), 1)
    keep = iota((rows * AUX, n_cols), 0) == (at // piece) * AUX
    col_sharp = jnp.sum(jnp.where(keep, spread, 0.0), axis=0, keepdims=True)
    keep = iota((rows * AUX, n_cols), 0) == (at // piece) * AUX + 1
    col_squares = jnp.sum(jnp.where(keep, spread, 0.0), axis=0, keepdims=True)
    labels = jnp.concatenate(split(first[:, :piece].reshape(n_cols, half)), axis=1)

    arrived(col_emb.at[twin], col_sem.at[twin])
    take(twin)
    for other in others_chip:
        slot = 2 * other + 1 - core
        arrived(col_emb.at[slot], col_sem.at[slot])
        take(slot)

    def product(c, labels):
        wide = quick(w_high[c], labels)
        return wide[:, :half] + wide[:, half:] + quick(w_low[c], labels[:, :half])

    def whole_product(labels):
        wide = quick(w_high[...].reshape(cols * pair, n_cols), labels)
        low = quick(w_low[...].reshape(cols * pair, n_cols), labels[:, :half])
        return (wide[:, :half] + wide[:, half:] + low).reshape(cols, pair, half)

    def block(c):
        ours = row_emb[c]
        both = jnp.concatenate(split(ours), axis=0)
        by_high, by_low = quick(both, c_high[...], 1), quick(both, c_low[...], 1)
        cross = by_high[:piece] + (by_high[piece:] + by_low[:piece] + by_low[piece:])
        squares = to_column(row_aux[c][1:2, :piece])
        row_sharp = to_column(row_aux[c][:1, :piece])
        distance = squares + col_squares - 2.0 * cross
        value = jnp.exp(-(distance * row_sharp * col_sharp)) * col_mask[pl.ds(c, 1)]
        tiles[c, core] = value
        push(tiles.at[c, core], tiles.at[c, core], tile_sem.at[c], (twin, z))

    def finish(c):
        arrived(tiles.at[c, 1 - core], tile_sem.at[c])
        value = tiles[c].reshape(pair, n_cols)
        w_high[c], w_low[c] = split(value)
        part[0, c, :pair] = product(c, labels)
        sums = to_line(jnp.sum(value, axis=1, keepdims=True))
        part[0, c, pair:, :pair] = jnp.broadcast_to(sums, (AUX, pair))

    def send_part(step, other, depth):
        push(
            part.at[step, other, pl.ds(0, depth)], summed.at[step, z, pl.ds(0, depth)],
            sum_sem.at[step, z], (r, other),
        )

    block(z)
    for i, other in enumerate(others_z):
        arrived(row_aux.at[other], aux_sem.at[other])
        arrived(row_emb.at[other], row_sem.at[other])
        block(other)
        before = others_z[i - 1] if i else z
        finish(before)
        if i:
            send_part(0, before, pair + AUX)
    if others_z:
        finish(others_z[-1])
        send_part(0, others_z[-1], pair + AUX)
    else:
        finish(z)

    kept = jnp.concatenate([first[2 * chip, :piece], first[2 * chip + 1, :piece]], axis=0)
    kept = 0.1 * kept
    scale = None
    for step in range(ITERS):
        if step > 0:
            labels = jnp.concatenate(split(later[step - 1].reshape(n_cols, half)), axis=1)
        if step < ITERS - 1:
            depth = pair + AUX if step == 0 else pair
            if step > 0:
                part[step, :, :pair] = whole_product(labels)
                for other in reversed(others_z):
                    send_part(step, other, depth)
            total = part[step, z, :depth]
            for other in others_z:
                arrived(summed.at[step, other, pl.ds(0, depth)], sum_sem.at[step, other])
                total = total + summed[step, other, :depth]
            if step == 0:
                scale = 0.9 / to_column(total[pair : pair + 1, :pair])
            later[step, chip] = total[:pair] * scale + kept
            for other in reversed(others_chip):
                push(
                    later.at[step, chip], later.at[step, chip], later_sem.at[step, chip],
                    (2 * other + core, z),
                )
            for other in others_chip:
                arrived(later.at[step, other], later_sem.at[step, other])
        else:
            last_part[...] = whole_product(labels).reshape(cols, 2, piece, half)
            for other in reversed(others_z):
                for k in range(2):
                    push(last_part.at[other, k], last.at[z, core], last_sem.at[z, core], (2 * chip + k, other))
            push(last_part.at[z, 1 - core], last.at[z, core], last_sem.at[z, core], (twin, z))
            last[z, core] = last_part[z, core]
            arrived(last.at[z, 1 - core], last_sem.at[z, 1 - core])
            for other in others_z:
                for k in range(2):
                    arrived(last.at[other, k], last_sem.at[other, k])
            total = jnp.sum(last[...], axis=0)
            own = jnp.where(core == 0, scale[:piece], scale[piece:])
            for k in range(2):
                out_ref[:, k * half : (k + 1) * half] = total[k] * own + 0.1 * send[k, :piece]
    for copy in sent:
        copy.wait_send()


def round_up(n, m):
    return (n + m - 1) // m * m


def local(chips, cols, embeddings, sharpness, soft_labels, seed_mask, tile_mask):
    piece, width = embeddings.shape
    half = soft_labels.shape[1] // 2
    rows = 2 * chips
    tile_rows, n_tiles = round_up(tile_mask.shape[0], 16), round_up(tile_mask.shape[1], 128)
    pair = 2 * piece
    sends = (
        (cols - 1) + (chips - 1) + 1 + 2 * (chips - 1) + 1 + (cols - 1) + (chips - 1) + cols
        + (ITERS - 1) * (cols + chips - 2) + 2 * cols - 1
    )
    f32, bf16, dma = jnp.float32, jnp.bfloat16, pltpu.SemaphoreType.DMA
    vmem = pl.BlockSpec(memory_space=pltpu.VMEM)
    return pl.pallas_call(
        functools.partial(kernel, chips, cols),
        out_shape=jax.ShapeDtypeStruct(soft_labels.shape, f32),
        in_specs=[pl.BlockSpec(memory_space=pltpu.HBM)] * 5,
        out_specs=vmem,
        scratch_shapes=[
            pltpu.VMEM((cols, piece, width), f32),
            pltpu.VMEM((rows, piece, width), f32),
            pltpu.VMEM((cols, AUX, 128), f32),
            pltpu.VMEM((tile_rows, n_tiles), f32),
            pltpu.VMEM((tile_rows, rows * piece), f32),
            pltpu.VMEM((rows, piece + AUX, half), f32),
            pltpu.VMEM((cols, 2, piece, rows * piece), f32),
            pltpu.VMEM((ITERS - 1, chips, pair, half), f32),
            pltpu.VMEM((ITERS - 1, cols, pair + AUX, half), f32),
            pltpu.VMEM((ITERS - 1, cols, pair + AUX, half), f32),
            pltpu.VMEM((cols, 2, piece, half), f32),
            pltpu.VMEM((cols, 2, piece, half), f32),
            pltpu.VMEM((cols, pair, rows * piece), bf16),
            pltpu.VMEM((cols, pair, rows * piece), bf16),
            pltpu.VMEM((rows * piece, width), bf16),
            pltpu.VMEM((rows * piece, width), bf16),
            pltpu.VMEM((2, piece + AUX, half), f32),
            pltpu.VMEM(soft_labels.shape, f32),
            pltpu.VMEM((1, piece), f32),
            pltpu.VMEM((1, piece), jnp.int32),
            pltpu.VMEM(tile_mask.shape, jnp.int32),
            dma((cols,)),
            dma((rows,)),
            dma((cols,)),
            dma((cols,)),
            dma((rows,)),
            dma((ITERS - 1, chips)),
            dma((ITERS - 1, cols)),
            dma((cols, 2)),
            dma((sends,)),
            dma((6,)),
        ],
        compiler_params=pltpu.CompilerParams(
            collective_id=0, has_side_effects=True, vmem_limit_bytes=60 * 1024 * 1024
        ),
    )(embeddings, sharpness.reshape(1, piece), soft_labels, seed_mask.reshape(1, piece), tile_mask)


def solution(mesh):
    return jax.shard_map(
        functools.partial(local, mesh.shape["row"] // 2, mesh.shape["col"]),
        mesh=mesh,
        in_specs=(
            P(("row", "col"), None),
            P(("row", "col")),
            P(("row", "col"), None),
            P(("row", "col")),
            P("row", None),
        ),
        out_specs=P(("row", "col"), None),
        check_vma=False,
    )
```
